256 devices in a mesh: col: 64 (over y, z_lo, x, core), row: 4 (over z_hi).
Axes of the slice: x: 4, y: 4, z: 8 (z_hi: 4, z_lo: 2; z = z_hi * 2 + z_lo), core: 2. Of those that a mesh axis runs over, the one named last changes fastest.
Arguments:
- root_inverse: float32 [2048, 2048], P('row', 'col')
- child_inverse: float32 [256, 512, 512], P(('col', 'row'))
- child_panel: float32 [256, 1024, 512], P(('col', 'row')), may hold values from -0.375 to 0.375
- structure: int32 [256, 8], P(('col', 'row')), may hold values from 0 to 15, as said below
- widths: int32 [256], P(('col', 'row')), may hold values from 256 to 512
Outputs:
- sigma_root: float32 [2048, 2048], P('row', 'col')
- child_cross: float32 [256, 1024, 512], P(('col', 'row'))
- child_variance: float32 [256, 512], P(('col', 'row'))
The draws below stay inside these ranges and needn't reach their ends.
Inputs may be any that keep to these rules, and one draw needn't show every extreme that they name: `structure`: each child names 8 distinct root blocks in rising order.
All inputs are finite; a program needn't handle non-finite values.
Results may differ from the reference program's by a relative error of at most 0.0003.
Values sent between devices are 32-bit elements; how exact they have to be, the bound alone decides.
No kernel may reach another device: no remote copies, remote signals or barrier semaphores. Data moves between devices by JAX's collectives and lax.ppermute only.
A program may use at most 192 MiB of HBM per device.

```python
import math
import jax
import jax.numpy as jnp
from jax import lax

TILE = 128
RT = 16
R = 2048
C = 512
KS = 8
NCH = 256


def draw_root_inverse(key, part):
    key = jax.random.fold_in(key, 5)
    first_key, second_key = jax.random.split(key)
    lower_part = jax.random.normal(first_key, (R, R)) * (1.0 / math.sqrt(R))
    diagonal = jnp.exp(jax.random.uniform(second_key, (R,), minval=math.log(0.5), maxval=math.log(2.0)))
    row_index = jnp.arange(R)[:, None]
    col_index = jnp.arange(R)[None, :]
    result = jnp.where(row_index > col_index, lower_part, 0.0) + jnp.where(row_index == col_index, diagonal[:, None], 0.0)
    return result.astype(jnp.float32)


def draw_child_inverse(key, part):
    key = jax.random.fold_in(key, 7)
    first_key, second_key = jax.random.split(key)
    lower_part = jax.random.normal(first_key, (NCH, C, C)) * (1.0 / math.sqrt(C))
    diagonal = jnp.exp(jax.random.uniform(second_key, (NCH, C, 1), minval=math.log(0.5), maxval=math.log(2.0)))
    row_index = jnp.arange(C)[None, :, None]
    col_index = jnp.arange(C)[None, None, :]
    result = jnp.where(row_index > col_index, lower_part, 0.0) + jnp.where(row_index == col_index, diagonal, 0.0)
    return result.astype(jnp.float32)


def draw_structure(key, part):
    key = jax.random.fold_in(key, 9)
    child_keys = jax.random.split(key, NCH)
    shuffled = jax.vmap(lambda single: jax.random.permutation(single, RT))(child_keys)
    return jnp.sort(shuffled[:, :KS], axis=1).astype(jnp.int32)


def draw_widths(key, part):
    key = jax.random.fold_in(key, 13)
    counts_drawn = jax.random.randint(key, (NCH,), C // 2, C + 1)
    return counts_drawn.at[0].set(C).astype(jnp.int32)


def shard_levels(own_key, extent, cuts, smallest, largest):
    gain, own = 1.0, jax.random.fold_in(own_key, 6)
    for position, shards_of in cuts:
        heights = jnp.exp(jax.random.uniform(jax.random.fold_in(own, position), (shards_of,), jnp.float32, smallest / len(cuts), largest / len(cuts)))
        gain = gain * jnp.repeat(heights, extent[position] // shards_of).reshape([-1 if axis == position else 1 for axis in range(len(extent))])
    return gain


def bell_draw(stream_key, dims, spread, reach, cuts=(), kind=jnp.bfloat16):
    entries = spread * jax.random.normal(stream_key, dims, jnp.float32)
    if cuts:
        entries = entries * shard_levels(stream_key, dims, cuts, -0.22, 0.18)
    return jnp.clip(entries, -reach, reach).astype(kind)


def setup_inputs(seed: int = 0) -> dict:
    keys = jax.random.split(jax.random.key(seed), 6)
    root_inverse = draw_root_inverse(jax.random.fold_in(keys[5], 71), 0)
    child_inverse = draw_child_inverse(jax.random.fold_in(keys[5], 71), 0)
    child_panel = bell_draw(keys[2], (NCH, KS * TILE, C), (KS * TILE // 4) ** -0.5, 0.375, ((0, 256),), jnp.float32)
    structure = draw_structure(jax.random.fold_in(keys[5], 71), 0)
    widths = draw_widths(jax.random.fold_in(keys[5], 71), 0)
    return {"root_inverse": root_inverse, "child_inverse": child_inverse, "child_panel": child_panel, "structure": structure, "widths": widths}


def one_child(covariance, inverse_block, panel_block, tiles, width_value):
    column_ids = jnp.arange(inverse_block.shape[0], dtype=jnp.int32)
    live_cols = (column_ids < width_value).astype(jnp.float32)
    masked_inverse = inverse_block * live_cols[:, None] * live_cols[None, :]
    masked_panel = panel_block * live_cols[None, :]
    ancestor_rows = (tiles[:, None] * TILE + jnp.arange(TILE, dtype=jnp.int32)[None, :]).reshape(-1).astype(jnp.int32)
    ancestor_block = jnp.take(jnp.take(covariance, ancestor_rows, axis=0), ancestor_rows, axis=1)
    update = jnp.dot(masked_panel, masked_inverse, precision=lax.Precision.HIGHEST, preferred_element_type=jnp.float32)
    cross_block = -jnp.dot(ancestor_block, update, precision=lax.Precision.HIGHEST, preferred_element_type=jnp.float32)
    variance = jnp.sum(masked_inverse * masked_inverse, axis=0) - jnp.sum(update * cross_block, axis=0)
    return cross_block, variance


def reference(root_inverse, child_inverse, child_panel, structure, widths):
    sigma_root = jnp.dot(root_inverse.T, root_inverse, precision=lax.Precision.HIGHEST, preferred_element_type=jnp.float32)

    def handle(items):
        return one_child(sigma_root, items[0], items[1], items[2], items[3])

    child_cross, child_variance = lax.map(handle, (child_inverse, child_panel, structure, widths))
    return sigma_root, child_cross, child_variance
```

```python
import itertools

import jax
import jax.numpy as jnp
from jax import lax
from jax.experimental import pallas as pl
from jax.experimental.pallas import tpu as pltpu
from jax.sharding import PartitionSpec as P

AXES = ("col", "row")
F32 = jnp.float32
BF16 = jnp.bfloat16
NN = (((1,), (0,)), ((), ()))
NT = (((1,), (1,)), ((), ()))


def flat(y, zl, x, c, zh):
    return (((y * 2 + zl) * 4 + x) * 2 + c) * 4 + zh


def places():
    return itertools.product(range(4), range(2), range(4), range(2), range(4))


def pairs(move):
    found = []
    for place in places():
        target = move(*place)
        if target is not None:
            found.append((flat(*place), flat(*target)))
    return found


def fold_move(y, zl, x, c, zh):
    target = {(0, 3): (3, 2), (0, 2): (3, 1), (1, 3): (2, 1)}.get((y, zh))
    return None if target is None else (target[0], zl, x, c, target[1])


def plane_move(step):
    return lambda y, zl, x, c, zh: (y, zl, x, c, (zh + step) % 4)


def pair_move(y, zl, x, c, zh):
    z = zh * 2 + zl
    near = z ^ 1 if c == 0 else (z + (1 if z % 2 else -1)) % 8
    return (y, near % 2, x, c, near // 2)


def first_move(step):
    def move(y, zl, x, c, zh):
        return ((y + step) % 4, zl, x, c, zh) if c == 0 else (y, zl, (x + step) % 4, c, zh)

    return move


def second_move(step):
    def move(y, zl, x, c, zh):
        return (y, zl, (x + step) % 4, c, zh) if c == 0 else ((y + step) % 4, zl, x, c, zh)

    return move


def core_move(y, zl, x, c, zh):
    return (y, zl, x, 1 - c, zh)


def send(value, move):
    return lax.ppermute(value, AXES, pairs(move))


def halves(value):
    high = value.astype(BF16)
    return high, (value - high.astype(F32)).astype(BF16)


def dot3(ah, al, bh, bl, dims):
    def one(a, b):
        return lax.dot_general(a, b, dims, preferred_element_type=F32)

    return one(ah, bh) + (one(ah, bl) + one(al, bh))


def update_kernel(width_ref, inverse_ref, panel_ref, high_ref, low_ref, square_ref):
    width = width_ref[0]
    inverse = inverse_ref[0]
    rows = lax.broadcasted_iota(jnp.int32, inverse.shape, 0)
    cols = lax.broadcasted_iota(jnp.int32, inverse.shape, 1)
    inverse = jnp.where((rows < width) & (cols < width), inverse, 0.0)
    square_ref[...] = jnp.sum(inverse * inverse, axis=0, keepdims=True)
    inverse_high, inverse_low = halves(inverse.T)
    for part in range(4):
        panel = panel_ref[0, pl.ds(part * 256, 256), :]
        live = lax.broadcasted_iota(jnp.int32, panel.shape, 1) < width
        panel_high, panel_low = halves(jnp.where(live, panel, 0.0))
        update = dot3(inverse_high, inverse_low, panel_high, panel_low, NT)
        high, low = halves(update)
        high_ref[:, pl.ds(part * 256, 256)] = high
        low_ref[:, pl.ds(part * 256, 256)] = low


def update(widths, child_inverse, child_panel):
    vmem = pl.BlockSpec(memory_space=pltpu.VMEM)
    return pl.pallas_call(
        update_kernel,
        out_shape=(
            jax.ShapeDtypeStruct((512, 1024), BF16),
            jax.ShapeDtypeStruct((512, 1024), BF16),
            jax.ShapeDtypeStruct((1, 512), F32),
        ),
        in_specs=[pl.BlockSpec(memory_space=pltpu.SMEM), vmem, vmem],
        out_specs=(vmem, vmem, vmem),
        compiler_params=pltpu.CompilerParams(vmem_limit_bytes=16 * 2**20),
        cost_estimate=pl.CostEstimate(flops=6 * 1024 * 512 * 512, bytes_accessed=5 * 2**20, transcendentals=0),
        name="update",
    )(widths, child_inverse, child_panel)


def final_kernel(
    where_ref, structure_ref, high_ref, low_ref, square_ref,
    q0, c10, c30, da0, db0, q1, c11, c31, da1, db1,
    cross_ref, variance_ref, sigma_ref,
    slot_ref, ah, al, sh, sl, oh, ol, th, tl, squares,
):
    y0, zl0, x0, core0, zh0 = (where_ref[i] for i in range(5))
    for block in range(16):
        slot_ref[block] = -1
    for t in range(8):
        slot_ref[structure_ref[0, t]] = t

    for t in range(8):
        superblock = structure_ref[0, t] // 4
        for r in range(3):
            @pl.when(superblock > r)
            def _():
                zero = jnp.zeros((128, 512), BF16)
                ah[pl.ds(t * 128, 128), pl.ds(r * 512, 512)] = zero
                al[pl.ds(t * 128, 128), pl.ds(r * 512, 512)] = zero
    for r in range(3):
        @pl.when(zh0 > r)
        def _():
            zero = jnp.zeros((512, 512), BF16)
            sh[:, pl.ds(r * 512, 512)] = zero
            sl[:, pl.ds(r * 512, 512)] = zero

        @pl.when(y0 > r)
        def _():
            zero = jnp.zeros((32, 512), BF16)
            oh[:, pl.ds(r * 512, 512)] = zero
            ol[:, pl.ds(r * 512, 512)] = zero

    def place(ref, count, base, d2, own):
        core = core0 if own else 1 - core0

        def step(i, carry):
            d1 = base + i // 2
            zr = i % 2
            y = jnp.where(core == 0, y0 - d1, y0 - d2) & 3
            x = jnp.where(core == 0, x0 - d2, x0 - d1) & 3
            zl = zl0 ^ zr
            inner = zl * 2 + x // 2
            part = (x & 1) * 2 + core
            mine = (zl == zl0) & (x == x0) & (core == core0)

            def segment(lane, size, group, k):
                slot = slot_ref[group * 4 + inner]

                def put(hi_ref, lo_ref, row):
                    high, low = halves(ref[i, :, pl.ds(lane, size)])
                    hi_ref[pl.ds(row, 32), pl.ds(k, size)] = high
                    lo_ref[pl.ds(row, 32), pl.ds(k, size)] = low

                @pl.when(slot >= 0)
                def _():
                    put(ah, al, pl.multiple_of(slot * 128 + part * 32, 32))

                @pl.when(zh0 == group)
                def _():
                    put(sh, sl, pl.multiple_of(inner * 128 + part * 32, 32))

                if own:
                    @pl.when(mine & (y0 == group))
                    def _():
                        put(oh, ol, 0)

            @pl.when(y == 0)
            def _():
                segment(0, 1280, 0, 0)

            @pl.when(y == 1)
            def _():
                segment(0, 1280, 1, 512)

            @pl.when(y == 2)
            def _():
                segment(0, 256, 1, 1792)
                segment(256, 1024, 2, 1024)

            @pl.when(y == 3)
            def _():
                segment(0, 768, 0, 1280)
                segment(768, 512, 3, 1536)

            return carry

        lax.fori_loop(0, count, step, 0)

    for own, (q, c1, c3, da, db) in ((True, (q0, c10, c30, da0, db0)), (False, (q1, c11, c31, da1, db1))):
        place(q, 8, 0, 0, own)
        place(c1, 8, 0, 1, own)
        place(c3, 8, 0, 3, own)
        place(da, 4, 0, 2, own)
        place(db, 4, 2, 2, own)

    squares[...] = jnp.zeros_like(squares)

    def times(r, carry):
        k = pl.multiple_of(r * 512, 512)
        live = jnp.int32(0)
        for q in range(4):
            live += (structure_ref[0, 2 * q] < 4 * (r + 1)).astype(jnp.int32)

        @pl.when(live == 0)
        def _():
            zero = jnp.zeros((512, 512), BF16)
            th[:, pl.ds(k, 512)] = zero
            tl[:, pl.ds(k, 512)] = zero

        for v in range(1, 5):
            @pl.when(live == v)
            def _():
                depth = 256 * v
                total = dot3(
                    high_ref[:, :depth], low_ref[:, :depth],
                    ah[:depth, pl.ds(k, 512)], al[:depth, pl.ds(k, 512)], NN,
                )
                high, low = halves(total)
                th[:, pl.ds(k, 512)] = high
                tl[:, pl.ds(k, 512)] = low
                square = total * total
                squares[...] += square[:, :128] + square[:, 128:256] + (square[:, 256:384] + square[:, 384:])

        return carry

    lax.fori_loop(0, 4, times, 0)

    def back(q, carry):
        row = pl.multiple_of(q * 256, 256)
        first = structure_ref[0, 2 * q] // 4
        for v in range(4):
            @pl.when(first == v)
            def _():
                k = 512 * v
                cross_ref[0, pl.ds(row, 256), :] = -dot3(
                    ah[pl.ds(row, 256), k:], al[pl.ds(row, 256), k:], th[:, k:], tl[:, k:], NT
                )

        return carry

    lax.fori_loop(0, 4, back, 0)
    variance_ref[...] = square_ref[...] + jnp.sum(squares[...].T, axis=0, keepdims=True)
    sigma_ref[...] = dot3(oh[...], ol[...], sh[...], sl[...], NT)


def final(where, structure, high, low, square, pieces):
    vmem = pl.BlockSpec(memory_space=pltpu.VMEM)
    smem = pl.BlockSpec(memory_space=pltpu.SMEM)
    return pl.pallas_call(
        final_kernel,
        out_shape=(
            jax.ShapeDtypeStruct((1, 1024, 512), F32),
            jax.ShapeDtypeStruct((1, 512), F32),
            jax.ShapeDtypeStruct((32, 512), F32),
        ),
        in_specs=[smem, smem] + [vmem] * 13,
        out_specs=(vmem, vmem, vmem),
        scratch_shapes=[
            pltpu.SMEM((16,), jnp.int32),
            pltpu.VMEM((1024, 2048), BF16), pltpu.VMEM((1024, 2048), BF16),
            pltpu.VMEM((512, 2048), BF16), pltpu.VMEM((512, 2048), BF16),
            pltpu.VMEM((32, 2048), BF16), pltpu.VMEM((32, 2048), BF16),
            pltpu.VMEM((512, 2048), BF16), pltpu.VMEM((512, 2048), BF16),
            pltpu.VMEM((512, 128), F32),
        ],
        compiler_params=pltpu.CompilerParams(vmem_limit_bytes=44 * 2**20),
        cost_estimate=pl.CostEstimate(flops=10**10, bytes_accessed=20 * 2**20, transcendentals=0),
        name="final",
    )(where, structure, high, low, square, *pieces)


def body(root_inverse, child_inverse, child_panel, structure, widths):
    col = lax.axis_index("col")
    zh0 = lax.axis_index("row")
    y0, zl0, x0, core0 = col // 16, (col // 8) % 2, (col // 2) % 4, col % 2
    where = jnp.stack([y0, zl0, x0, core0, zh0]).astype(jnp.int32)
    high, low, square = update(widths, child_inverse, child_panel)

    own = root_inverse.T
    folded = send(own, fold_move)
    moved = ((y0 == 3) & ((zh0 == 1) | (zh0 == 2))) | ((y0 == 2) & (zh0 == 1))
    own = jnp.where(moved, folded, own)
    planes = jnp.stack([own, send(own, plane_move(1)), send(own, plane_move(2)), send(own, plane_move(3))])
    base = jnp.where(y0 == 0, 0, 1)
    wide = jnp.concatenate([planes[(zh0 - base - s) % 4] for s in range(3)], axis=1)
    line = lax.dynamic_slice(wide, (0, jnp.where(y0 >= 2, 256, 0)), (32, 1280))
    both = jnp.stack([line, send(line, pair_move)])
    quad = jnp.concatenate(
        [both, send(both, first_move(1)), send(both, first_move(2)), send(both, first_move(3))], axis=0
    )
    from_left = send(quad, second_move(1))
    from_right = send(quad, second_move(3))
    far_a = send(from_left[:4], second_move(1))
    far_b = send(from_right[4:], second_move(3))
    mine = [quad, from_left, from_right, far_a, far_b]
    others = [send(piece, core_move) for piece in mine]
    cross, variance, sigma = final(where, structure, high, low, square, mine + others)
    return sigma.T, cross, variance


def solution(mesh):
    placed = (
        P("row", "col"),
        P(("col", "row"), None, None),
        P(("col", "row"), None, None),
        P(("col", "row"), None),
        P(("col", "row")),
    )
    return jax.shard_map(
        body,
        mesh=mesh,
        in_specs=placed,
        out_specs=(P("row", "col"), P(("col", "row"), None, None), P(("col", "row"), None)),
        check_vma=False,
    )
```

```python
import itertools

import jax
import jax.numpy as jnp
from jax import lax
from jax.experimental import pallas as pl
from jax.experimental.pallas import tpu as pltpu
from jax.sharding import PartitionSpec as P

AXES = ("col", "row")
F32 = jnp.float32
BF16 = jnp.bfloat16
NN = (((1,), (0,)), ((), ()))
NT = (((1,), (1,)), ((), ()))


def flat(y, zl, x, c, zh):
    return (((y * 2 + zl) * 4 + x) * 2 + c) * 4 + zh


def places():
    return itertools.product(range(4), range(2), range(4), range(2), range(4))


def pairs(move):
    found = []
    for place in places():
        target = move(*place)
        if target is not None:
            found.append((flat(*place), flat(*target)))
    return found


def fold_move(y, zl, x, c, zh):
    target = {(0, 1): (3, 1), (0, 2): (3, 2), (1, 2): (2, 1)}.get((y, zh))
    return None if target is None else (target[0], zl, x, c, target[1])


def plane_move(step):
    return lambda y, zl, x, c, zh: (y, zl, x, c, (zh + step) % 4)


def pair_move(y, zl, x, c, zh):
    z = zh * 2 + zl
    near = z ^ 1 if c == 0 else (z + (1 if z % 2 else -1)) % 8
    return (y, near % 2, x, c, near // 2)


def first_move(step):
    def move(y, zl, x, c, zh):
        return ((y + step) % 4, zl, x, c, zh) if c == 0 else (y, zl, (x + step) % 4, c, zh)

    return move


def second_move(step):
    def move(y, zl, x, c, zh):
        return (y, zl, (x + step) % 4, c, zh) if c == 0 else ((y + step) % 4, zl, x, c, zh)

    return move


def core_move(y, zl, x, c, zh):
    return (y, zl, x, 1 - c, zh)


def send(value, move):
    return lax.ppermute(value, AXES, pairs(move))


def halves(value):
    high = value.astype(BF16)
    return high, (value - high.astype(F32)).astype(BF16)


def dot3(ah, al, bh, bl, dims):
    def one(a, b):
        return lax.dot_general(a, b, dims, preferred_element_type=F32)

    return one(ah, bh) + (one(ah, bl) + one(al, bh))


def update_kernel(width_ref, inverse_ref, panel_ref, high_ref, low_ref, square_ref):
    width = width_ref[0]
    inverse = inverse_ref[0]
    rows = lax.broadcasted_iota(jnp.int32, inverse.shape, 0)
    cols = lax.broadcasted_iota(jnp.int32, inverse.shape, 1)
    inverse = jnp.where((rows < width) & (cols < width), inverse, 0.0)
    square_ref[...] = jnp.sum(inverse * inverse, axis=0, keepdims=True)
    inverse_high, inverse_low = halves(inverse.T)
    for part in range(4):
        panel = panel_ref[0, pl.ds(part * 256, 256), :]
        live = lax.broadcasted_iota(jnp.int32, panel.shape, 1) < width
        panel_high, panel_low = halves(jnp.where(live, panel, 0.0))
        update = dot3(inverse_high, inverse_low, panel_high, panel_low, NT)
        high, low = halves(update)
        high_ref[:, pl.ds(part * 256, 256)] = high
        low_ref[:, pl.ds(part * 256, 256)] = low


def update(widths, child_inverse, child_panel):
    vmem = pl.BlockSpec(memory_space=pltpu.VMEM)
    return pl.pallas_call(
        update_kernel,
        out_shape=(
            jax.ShapeDtypeStruct((512, 1024), BF16),
            jax.ShapeDtypeStruct((512, 1024), BF16),
            jax.ShapeDtypeStruct((1, 512), F32),
        ),
        in_specs=[pl.BlockSpec(memory_space=pltpu.SMEM), vmem, vmem],
        out_specs=(vmem, vmem, vmem),
        compiler_params=pltpu.CompilerParams(vmem_limit_bytes=16 * 2**20),
        cost_estimate=pl.CostEstimate(flops=6 * 1024 * 512 * 512, bytes_accessed=5 * 2**20, transcendentals=0),
        name="update",
    )(widths, child_inverse, child_panel)


VMEM = pl.BlockSpec(memory_space=pltpu.VMEM)
SMEM = pl.BlockSpec(memory_space=pltpu.SMEM)
EARLY, LATE = 768, 512


def line_kernel(where_ref, *refs):
    out = refs[-1]
    y0, zh0 = where_ref[0], where_ref[4]
    whole = jnp.minimum(y0, 2)
    half = jnp.where(y0 == 1, 2, 1)
    for d in range(4):
        source = refs[d]
        slot = (zh0 - d) & 3

        @pl.when(slot == 3)
        def _():
            out[:, EARLY:] = source[...]

        @pl.when((slot == whole) & (y0 < 2))
        def _():
            out[:, :512] = source[...]

        @pl.when((slot == half) & (y0 < 2))
        def _():
            out[:, 512:EARLY] = source[:, :256]

        @pl.when((slot == whole) & (y0 >= 2))
        def _():
            out[:, 256:EARLY] = source[...]

        @pl.when((slot == half) & (y0 >= 2))
        def _():
            out[:, :256] = source[:, 256:]


def make_line(where, planes):
    return pl.pallas_call(
        line_kernel,
        out_shape=jax.ShapeDtypeStruct((32, EARLY + LATE), F32),
        in_specs=[SMEM] + [VMEM] * 4,
        out_specs=VMEM,
        name="line",
    )(where, *planes)


def quad_kernel(*refs):
    early, late = refs[-2:]
    for d in range(4):
        early[2 * d : 2 * d + 2] = refs[d][:, :, :EARLY]
        late[2 * d : 2 * d + 2] = refs[d][:, :, EARLY:]


def make_quads(parts):
    return pl.pallas_call(
        quad_kernel,
        out_shape=(
            jax.ShapeDtypeStruct((8, 32, EARLY), F32),
            jax.ShapeDtypeStruct((8, 32, LATE), F32),
        ),
        in_specs=[VMEM] * 4,
        out_specs=(VMEM, VMEM),
        name="quads",
    )(*parts)


def join_kernel(*refs):
    out = refs[-1]
    start = 0
    for source in refs[:-1]:
        out[start : start + source.shape[0]] = source[...]
        start += source.shape[0]


def join(parts):
    count = sum(part.shape[0] for part in parts)
    return pl.pallas_call(
        join_kernel,
        out_shape=jax.ShapeDtypeStruct((count,) + parts[0].shape[1:], F32),
        in_specs=[VMEM] * len(parts),
        out_specs=VMEM,
        name="join",
    )(*parts)


def place_all(where_ref, slot_ref, pieces, segments, outs):
    y0, zl0, x0, core0, zh0 = (where_ref[i] for i in range(5))
    ah, al, sh, sl, oh, ol = outs
    near, left, right, far, other, other_far = pieces

    def place(ref, offset, d2, core):
        def step(i, carry):
            d1 = i // 2
            y = jnp.where(core == 0, y0 - d1, y0 - d2) & 3
            x = jnp.where(core == 0, x0 - d2, x0 - d1) & 3
            zl = zl0 ^ (i & 1)
            inner = zl * 2 + x // 2
            part = (x & 1) * 2 + core
            mine = (zl == zl0) & (x == x0) & (core == core0)

            def segment(lane, size, group, k):
                slot = slot_ref[group * 4 + inner]

                def put(hi_ref, lo_ref, row):
                    high, low = halves(ref[offset + i, :, pl.ds(lane, size)])
                    hi_ref[pl.ds(row, 32), pl.ds(k, size)] = high
                    lo_ref[pl.ds(row, 32), pl.ds(k, size)] = low

                @pl.when(slot >= 0)
                def _():
                    put(ah, al, pl.multiple_of(slot * 128 + part * 32, 32))

                @pl.when(zh0 == group)
                def _():
                    put(sh, sl, pl.multiple_of(inner * 128 + part * 32, 32))

                @pl.when(mine & (y0 == group))
                def _():
                    put(oh, ol, 0)

            for group in range(4):
                @pl.when(y == group)
                def _():
                    for found in segments[group]:
                        segment(*found)

            return carry

        lax.fori_loop(0, 8, step, 0)

    place(near, 0, 0, core0)
    place(left, 0, 1, core0)
    place(right, 0, 3, core0)
    place(far, 0, 2, core0)
    for index, d2 in enumerate((0, 1, 3)):
        place(other, 8 * index, d2, 1 - core0)
    place(other_far, 0, 2, 1 - core0)


def fill_slots(structure_ref, slot_ref):
    for block in range(16):
        slot_ref[block] = -1
    for t in range(8):
        slot_ref[structure_ref[0, t]] = t


def fold_squares(square):
    return square[:, :128] + square[:, 128:256] + (square[:, 256:384] + square[:, 384:])


EARLY_SEGMENTS = (
    ((0, 768, 0, 0),),
    ((0, 768, 1, 512),),
    ((0, 256, 1, 1280), (256, 512, 2, 1024)),
    ((0, 768, 0, 768),),
)
LATE_SEGMENTS = tuple(((0, 512, group, 0),) for group in range(4))


def early_kernel(
    where_ref, structure_ref, high_ref, low_ref, q, c1, c3, d, e1, e2,
    ah, al, th, tl, squares, sigma_ref, slot_ref, sh, sl, oh, ol,
):
    y0, zh0 = where_ref[0], where_ref[4]
    fill_slots(structure_ref, slot_ref)
    for t in range(8):
        superblock = structure_ref[0, t] // 4
        for r in range(3):
            @pl.when(superblock > r)
            def _():
                zero = jnp.zeros((128, 512), BF16)
                ah[pl.ds(t * 128, 128), pl.ds(r * 512, 512)] = zero
                al[pl.ds(t * 128, 128), pl.ds(r * 512, 512)] = zero
    for r in range(3):
        @pl.when(zh0 > r)
        def _():
            zero = jnp.zeros((512, 512), BF16)
            sh[:, pl.ds(r * 512, 512)] = zero
            sl[:, pl.ds(r * 512, 512)] = zero

        @pl.when(y0 > r)
        def _():
            zero = jnp.zeros((32, 512), BF16)
            oh[:, pl.ds(r * 512, 512)] = zero
            ol[:, pl.ds(r * 512, 512)] = zero

    place_all(where_ref, slot_ref, (q, c1, c3, d, e1, e2), EARLY_SEGMENTS, (ah, al, sh, sl, oh, ol))
    squares[...] = jnp.zeros_like(squares)

    def times(r, carry):
        k = pl.multiple_of(r * 512, 512)
        live = jnp.int32(0)
        for q in range(4):
            live += (structure_ref[0, 2 * q] < 4 * (r + 1)).astype(jnp.int32)

        @pl.when(live == 0)
        def _():
            zero = jnp.zeros((512, 512), BF16)
            th[:, pl.ds(k, 512)] = zero
            tl[:, pl.ds(k, 512)] = zero

        for v in range(1, 5):
            @pl.when(live == v)
            def _():
                depth = 256 * v
                total = dot3(
                    high_ref[:, :depth], low_ref[:, :depth],
                    ah[:depth, pl.ds(k, 512)], al[:depth, pl.ds(k, 512)], NN,
                )
                high, low = halves(total)
                th[:, pl.ds(k, 512)] = high
                tl[:, pl.ds(k, 512)] = low
                squares[...] += fold_squares(total * total)

        return carry

    lax.fori_loop(0, 3, times, 0)
    sigma_ref[...] = dot3(sh[...], sl[...], oh[...], ol[...], NT).T


def early(where, structure, high, low, pieces):
    return pl.pallas_call(
        early_kernel,
        out_shape=(
            jax.ShapeDtypeStruct((1024, 1536), BF16), jax.ShapeDtypeStruct((1024, 1536), BF16),
            jax.ShapeDtypeStruct((512, 1536), BF16), jax.ShapeDtypeStruct((512, 1536), BF16),
            jax.ShapeDtypeStruct((512, 128), F32), jax.ShapeDtypeStruct((32, 512), F32),
        ),
        in_specs=[SMEM, SMEM] + [VMEM] * 8,
        out_specs=(VMEM,) * 6,
        scratch_shapes=[
            pltpu.SMEM((16,), jnp.int32),
            pltpu.VMEM((512, 1536), BF16), pltpu.VMEM((512, 1536), BF16),
            pltpu.VMEM((32, 1536), BF16), pltpu.VMEM((32, 1536), BF16),
        ],
        compiler_params=pltpu.CompilerParams(vmem_limit_bytes=30 * 2**20),
        cost_estimate=pl.CostEstimate(flops=5 * 10**9, bytes_accessed=10 * 2**20, transcendentals=0),
        name="early",
    )(where, structure, high, low, *pieces)


def middle_kernel(structure_ref, ah, al, th, tl, cross_ref):
    def back(q, carry):
        row = pl.multiple_of(q * 256, 256)
        first = structure_ref[0, 2 * q] // 4
        for v in range(3):
            @pl.when(first == v)
            def _():
                k = 512 * v
                cross_ref[pl.ds(row, 256), :] = dot3(
                    ah[pl.ds(row, 256), k:], al[pl.ds(row, 256), k:], th[:, k:], tl[:, k:], NT
                )

        @pl.when(first == 3)
        def _():
            cross_ref[pl.ds(row, 256), :] = jnp.zeros((256, 512), F32)

        return carry

    lax.fori_loop(0, 4, back, 0)


def middle(structure, ah, al, th, tl):
    return pl.pallas_call(
        middle_kernel,
        out_shape=jax.ShapeDtypeStruct((1024, 512), F32),
        in_specs=[SMEM] + [VMEM] * 4,
        out_specs=VMEM,
        compiler_params=pltpu.CompilerParams(vmem_limit_bytes=20 * 2**20),
        cost_estimate=pl.CostEstimate(flops=4 * 10**9, bytes_accessed=10 * 2**20, transcendentals=0),
        name="middle",
    )(structure, ah, al, th, tl)


def late_kernel(
    where_ref, structure_ref, high_ref, low_ref, square_ref, squares_ref, before_ref, partial_ref,
    q, c1, c3, d, e1, e2,
    cross_ref, variance_ref, sigma_ref, slot_ref, ah, al, th, tl, sh, sl, oh, ol,
):
    fill_slots(structure_ref, slot_ref)
    place_all(where_ref, slot_ref, (q, c1, c3, d, e1, e2), LATE_SEGMENTS, (ah, al, sh, sl, oh, ol))
    total = dot3(high_ref[...], low_ref[...], ah[...], al[...], NN)
    high, low = halves(total)
    th[...] = high
    tl[...] = low
    squares = squares_ref[...] + fold_squares(total * total)
    variance_ref[...] = square_ref[...] + jnp.sum(squares.T, axis=0, keepdims=True)

    def back(q, carry):
        row = pl.multiple_of(q * 256, 256)
        cross_ref[0, pl.ds(row, 256), :] = -(
            before_ref[pl.ds(row, 256), :]
            + dot3(ah[pl.ds(row, 256), :], al[pl.ds(row, 256), :], th[...], tl[...], NT)
        )
        return carry

    lax.fori_loop(0, 4, back, 0)
    sigma_ref[...] = partial_ref[...] + dot3(sh[...], sl[...], oh[...], ol[...], NT).T


def late(where, structure, high, low, square, squares, before, partial, pieces):
    return pl.pallas_call(
        late_kernel,
        out_shape=(
            jax.ShapeDtypeStruct((1, 1024, 512), F32),
            jax.ShapeDtypeStruct((1, 512), F32),
            jax.ShapeDtypeStruct((32, 512), F32),
        ),
        in_specs=[SMEM, SMEM] + [VMEM] * 12,
        out_specs=(VMEM, VMEM, VMEM),
        scratch_shapes=[
            pltpu.SMEM((16,), jnp.int32),
            pltpu.VMEM((1024, 512), BF16), pltpu.VMEM((1024, 512), BF16),
            pltpu.VMEM((512, 512), BF16), pltpu.VMEM((512, 512), BF16),
            pltpu.VMEM((512, 512), BF16), pltpu.VMEM((512, 512), BF16),
            pltpu.VMEM((32, 512), BF16), pltpu.VMEM((32, 512), BF16),
        ],
        compiler_params=pltpu.CompilerParams(vmem_limit_bytes=26 * 2**20),
        cost_estimate=pl.CostEstimate(flops=4 * 10**9, bytes_accessed=10 * 2**20, transcendentals=0),
        name="late",
    )(where, structure, high, low, square, squares, before, partial, *pieces)


def body(root_inverse, child_inverse, child_panel, structure, widths):
    tie = lax.optimization_barrier
    col = lax.axis_index("col")
    zh0 = lax.axis_index("row")
    y0, zl0, x0, core0 = col // 16, (col // 8) % 2, (col // 2) % 4, col % 2
    where = jnp.stack([y0, zl0, x0, core0, zh0]).astype(jnp.int32)

    own = root_inverse.T
    folded = send(own, fold_move)
    moved = ((y0 == 3) & ((zh0 == 1) | (zh0 == 2))) | ((y0 == 2) & (zh0 == 1))
    own = jnp.where(moved, folded, own)
    planes = [own] + [send(own, plane_move(step)) for step in (1, 2, 3)]
    line = make_line(where, planes)
    both = jnp.stack([line, send(line, pair_move)])
    crossed = [send(both, first_move(step)) for step in (1, 2, 3)]
    both, child_inverse, child_panel = tie((both, child_inverse, child_panel))
    high, low, square = update(widths, child_inverse, child_panel)
    crossed, high, low, square = tie((crossed, high, low, square))
    quad_e, quad_l = make_quads([both] + crossed)

    left_e, right_e = send(quad_e, second_move(1)), send(quad_e, second_move(3))
    far_e = [send(left_e[:4], second_move(1)), send(right_e[4:], second_move(3))]
    quad_l, left_e, right_e = tie((quad_l, left_e, right_e))
    left_l, right_l = send(quad_l, second_move(1)), send(quad_l, second_move(3))
    other_e = send(join([quad_e, left_e, right_e]), core_move)
    far_e = join(far_e)
    other_far_e = send(far_e, core_move)

    far_l = [send(left_l[:4], second_move(1)), send(right_l[4:], second_move(3))]
    other_l = send(join([quad_l, left_l, right_l]), core_move)
    other_far_e, left_l, right_l = tie((other_far_e, left_l, right_l))
    ah, al, th, tl, squares, partial = early(
        where, structure, high, low, [quad_e, left_e, right_e, far_e, other_e, other_far_e]
    )
    far_l, ah = tie((far_l, ah))
    far_l = join(far_l)
    other_far_l = send(far_l, core_move)
    before = middle(structure, ah, al, th, tl)
    cross, variance, sigma = late(
        where, structure, high, low, square, squares, before, partial,
        [quad_l, left_l, right_l, far_l, other_l, other_far_l],
    )
    return sigma.T, cross, variance


def solution(mesh):
    placed = (
        P("row", "col"),
        P(("col", "row"), None, None),
        P(("col", "row"), None, None),
        P(("col", "row"), None),
        P(("col", "row")),
    )
    return jax.shard_map(
        body,
        mesh=mesh,
        in_specs=placed,
        out_specs=(P("row", "col"), P(("col", "row"), None, None), P(("col", "row"), None)),
        check_vma=False,
    )
```

```python
import itertools

import jax
import jax.numpy as jnp
from jax import lax
from jax.experimental import pallas as pl
from jax.experimental.pallas import tpu as pltpu
from jax.sharding import PartitionSpec as P

AXES = ("col", "row")
F32 = jnp.float32
BF16 = jnp.bfloat16
NN = (((1,), (0,)), ((), ()))
NT = (((1,), (1,)), ((), ()))


def flat(y, zl, x, c, zh):
    return (((y * 2 + zl) * 4 + x) * 2 + c) * 4 + zh


def places():
    return itertools.product(range(4), range(2), range(4), range(2), range(4))


def pairs(move):
    found = []
    for place in places():
        target = move(*place)
        if target is not None:
            found.append((flat(*place), flat(*target)))
    return found


def fold_move(y, zl, x, c, zh):
    target = {(0, 1): (3, 1), (0, 2): (3, 2), (1, 2): (2, 1)}.get((y, zh))
    return None if target is None else (target[0], zl, x, c, target[1])


def plane_move(step):
    return lambda y, zl, x, c, zh: (y, zl, x, c, (zh + step) % 4)


def pair_move(y, zl, x, c, zh):
    z = zh * 2 + zl
    near = z ^ 1 if c == 0 else (z + (1 if z % 2 else -1)) % 8
    return (y, near % 2, x, c, near // 2)


def first_move(step):
    def move(y, zl, x, c, zh):
        return ((y + step) % 4, zl, x, c, zh) if c == 0 else (y, zl, (x + step) % 4, c, zh)

    return move


def second_move(step):
    def move(y, zl, x, c, zh):
        return (y, zl, (x + step) % 4, c, zh) if c == 0 else ((y + step) % 4, zl, x, c, zh)

    return move


def core_move(y, zl, x, c, zh):
    return (y, zl, x, 1 - c, zh)


def send(value, move):
    return lax.ppermute(value, AXES, pairs(move))


def halves(value):
    high = value.astype(BF16)
    return high, (value - high.astype(F32)).astype(BF16)


def dot3(ah, al, bh, bl, dims):
    def one(a, b):
        return lax.dot_general(a, b, dims, preferred_element_type=F32)

    return one(ah, bh) + (one(ah, bl) + one(al, bh))


def update_kernel(width_ref, inverse_ref, panel_ref, high_ref, low_ref, square_ref):
    width = width_ref[0]
    inverse = inverse_ref[0]
    rows = lax.broadcasted_iota(jnp.int32, inverse.shape, 0)
    cols = lax.broadcasted_iota(jnp.int32, inverse.shape, 1)
    inverse = jnp.where((rows < width) & (cols < width), inverse, 0.0)
    square_ref[...] = jnp.sum(inverse * inverse, axis=0, keepdims=True)
    inverse_high, inverse_low = halves(inverse.T)
    for part in range(4):
        panel = panel_ref[0, pl.ds(part * 256, 256), :]
        live = lax.broadcasted_iota(jnp.int32, panel.shape, 1) < width
        panel_high, panel_low = halves(jnp.where(live, panel, 0.0))
        update = dot3(inverse_high, inverse_low, panel_high, panel_low, NT)
        high, low = halves(update)
        high_ref[:, pl.ds(part * 256, 256)] = high
        low_ref[:, pl.ds(part * 256, 256)] = low


def update(widths, child_inverse, child_panel):
    vmem = pl.BlockSpec(memory_space=pltpu.VMEM)
    return pl.pallas_call(
        update_kernel,
        out_shape=(
            jax.ShapeDtypeStruct((512, 1024), BF16),
            jax.ShapeDtypeStruct((512, 1024), BF16),
            jax.ShapeDtypeStruct((1, 512), F32),
        ),
        in_specs=[pl.BlockSpec(memory_space=pltpu.SMEM), vmem, vmem],
        out_specs=(vmem, vmem, vmem),
        compiler_params=pltpu.CompilerParams(vmem_limit_bytes=12 * 2**20),
        cost_estimate=pl.CostEstimate(flops=6 * 1024 * 512 * 512, bytes_accessed=5 * 2**20, transcendentals=0),
        name="update",
    )(widths, child_inverse, child_panel)


VMEM = pl.BlockSpec(memory_space=pltpu.VMEM)
SMEM = pl.BlockSpec(memory_space=pltpu.SMEM)
EARLY, LATE = 768, 512
WIDE = EARLY + LATE


def limit(mebibytes):
    return pltpu.CompilerParams(vmem_limit_bytes=mebibytes * 2**20)


def line_kernel(where_ref, *refs):
    out = refs[-1]
    y0, zh0 = where_ref[0], where_ref[4]
    whole = jnp.minimum(y0, 2)
    half = jnp.where(y0 == 1, 2, 1)
    for d in range(4):
        source = refs[d]
        slot = (zh0 - d) & 3

        @pl.when(slot == 3)
        def _():
            out[:, EARLY:] = source[...]

        @pl.when((slot == whole) & (y0 < 2))
        def _():
            out[:, :512] = source[...]

        @pl.when((slot == half) & (y0 < 2))
        def _():
            out[:, 512:EARLY] = source[:, :256]

        @pl.when((slot == whole) & (y0 >= 2))
        def _():
            out[:, 256:EARLY] = source[...]

        @pl.when((slot == half) & (y0 >= 2))
        def _():
            out[:, :256] = source[:, 256:]


def make_line(where, planes):
    return pl.pallas_call(
        line_kernel,
        out_shape=jax.ShapeDtypeStruct((32, WIDE), F32),
        in_specs=[SMEM] + [VMEM] * 4,
        out_specs=VMEM,
        compiler_params=limit(2),
        name="line",
    )(where, *planes)


def join_kernel(*refs):
    out = refs[-1]
    start = 0
    for source in refs[:-1]:
        count = source.shape[0] if len(source.shape) == 3 else 1
        out[start : start + count] = source[...].reshape((count,) + out.shape[1:])
        start += count


def join(parts):
    count = sum(part.shape[0] if part.ndim == 3 else 1 for part in parts)
    return pl.pallas_call(
        join_kernel,
        out_shape=jax.ShapeDtypeStruct((count,) + parts[0].shape[-2:], F32),
        in_specs=[VMEM] * len(parts),
        out_specs=VMEM,
        compiler_params=limit(6),
        name="join",
    )(*parts)


def mix_kernel(left, right, quad, ahead, behind, aside):
    ahead[:2] = left[:2]
    ahead[2:] = quad[:2]
    behind[:2] = right[2:]
    behind[2:] = quad[2:]
    aside[:2] = left[2:]
    aside[2:] = right[:2]


def mix(left, right, quad):
    shape = jax.ShapeDtypeStruct((4, 32, WIDE), F32)
    return pl.pallas_call(
        mix_kernel,
        out_shape=(shape,) * 3,
        in_specs=[VMEM] * 3,
        out_specs=(VMEM,) * 3,
        compiler_params=limit(5),
        name="mix",
    )(left, right, quad)


def tails_kernel(ahead, behind, ahead_out, behind_out):
    ahead_out[...] = ahead[2:]
    behind_out[...] = behind[2:]


def tails(ahead, behind):
    shape = jax.ShapeDtypeStruct((2, 32, WIDE), F32)
    return pl.pallas_call(
        tails_kernel,
        out_shape=(shape,) * 2,
        in_specs=[VMEM] * 2,
        out_specs=(VMEM,) * 2,
        compiler_params=limit(4),
        name="tails",
    )(ahead, behind)


ROWS = 13 * 128
PLAN = (
    ((0, 768, 0, 0), (0, 768, 3, 768), (768, 512, 0, 1536)),
    ((0, 768, 1, 512), (0, 256, 2, 1280), (768, 512, 1, 1536)),
    ((256, 512, 2, 1024), (768, 512, 2, 1536)),
    ((768, 512, 3, 1536),),
)


def source_of(zr, d2, d1):
    if zr == 0:
        if d2 == 2:
            return (1, d1) if d1 < 2 else (1, 2 + d1)
        return 0, {0: 0, 1: 4, 3: 8}[d2] + d1
    if d2 == 0:
        return 0, 12 + d1
    if d2 == 1:
        return (1, 2 + d1) if d1 < 2 else (1, 6 + d1)
    if d2 == 3:
        return (1, 10 + d1) if d1 < 2 else (1, 4 + d1)
    return 2, d1


def lay_kernel(where_ref, structure_ref, near, side, other_near, other_side, ah, al, block_ref, table_ref):
    y0, zl0, x0, core0, zh0 = (where_ref[i] for i in range(5))
    for t in range(8):
        block_ref[t] = structure_ref[0, t]
    for t in range(4):
        block_ref[8 + t] = zh0 * 4 + t
    block_ref[12] = y0 * 4 + zl0 * 2 + x0 // 2
    for zr, d2, d1 in itertools.product(range(2), range(4), range(4)):
        array, index = source_of(zr, d2, d1)
        table_ref[zr * 16 + d2 * 4 + d1] = array * 16 + index

    def fill(*sources):
        def step(t, carry):
            block = block_ref[t]
            y, inner = block // 4, block & 3
            zr, xb = (inner // 2) ^ zl0, (inner & 1) * 2
            base = pl.multiple_of(t * 128, 128)

            def copy(part, lane, size, group, k):
                core = part & 1
                dy, dx = (y0 - group) & 3, (x0 - xb - part // 2) & 3
                d1, d2 = (dy, dx) if core == 0 else (dx, dy)
                first, second = sources[core]
                code = table_ref[zr * 16 + d2 * 4 + d1]
                index = code & 15
                lanes = slice(lane, lane + size)
                value = jnp.where(
                    code < 16, first[index, :, lanes], second[jnp.minimum(index, 11), :, lanes]
                )
                high, low = halves(value)
                row = pl.multiple_of(base + part * 32, 32)
                ah[pl.ds(row, 32), k : k + size] = high
                al[pl.ds(row, 32), k : k + size] = low

            for superblock in range(4):
                @pl.when(y == superblock)
                def _():
                    if superblock:
                        zero = jnp.zeros((128, 512 * superblock), BF16)
                        ah[pl.ds(base, 128), : 512 * superblock] = zero
                        al[pl.ds(base, 128), : 512 * superblock] = zero
                    for part in range(4):
                        for found in PLAN[superblock]:
                            copy(part, *found)

            return carry

        lax.fori_loop(0, 13, step, 0)

    @pl.when(core0 == 0)
    def _():
        fill((near, side), (other_near, other_side))

    @pl.when(core0 == 1)
    def _():
        fill((other_near, other_side), (near, side))


def lay(where, structure, pieces):
    shape = jax.ShapeDtypeStruct((ROWS, 2048), BF16)
    return pl.pallas_call(
        lay_kernel,
        out_shape=(shape, shape),
        in_specs=[SMEM, SMEM] + [VMEM] * 4,
        out_specs=(VMEM, VMEM),
        scratch_shapes=[pltpu.SMEM((16,), jnp.int32), pltpu.SMEM((32,), jnp.int32)],
        compiler_params=limit(25),
        cost_estimate=pl.CostEstimate(flops=10**10, bytes_accessed=10 * 2**20, transcendentals=0),
        name="lay",
    )(where, structure, *pieces)


FAR_PLAN = (
    ((0, 768, 0, 0), (768, 512, 0, 1536)),
    ((0, 768, 1, 512), (768, 512, 1, 1536)),
    ((0, 256, 1, 1280), (256, 512, 2, 1024), (768, 512, 2, 1536)),
    ((0, 768, 0, 768), (768, 512, 3, 1536)),
)


def patch(where_ref, structure_ref, slot_ref, far, other_far, ah, al):
    y0, zl0, x0, core0, zh0 = (where_ref[i] for i in range(5))
    for block in range(16):
        slot_ref[block] = -1
    for t in range(8):
        slot_ref[structure_ref[0, t]] = t

    def fill(source, core):
        def step(d1, carry):
            y = (y0 - jnp.where(core == 0, d1, 2)) & 3
            x = (x0 - jnp.where(core == 0, 2, d1)) & 3
            inner = (1 - zl0) * 2 + x // 2
            offset = (x & 1) * 64 + core * 32
            for group in range(4):
                @pl.when(y == group)
                def _():
                    for lane, size, superblock, k in FAR_PLAN[group]:
                        slot = slot_ref[superblock * 4 + inner]

                        def put(block):
                            row = pl.multiple_of(block * 128 + offset, 32)
                            high, low = halves(source[d1, :, lane : lane + size])
                            ah[pl.ds(row, 32), k : k + size] = high
                            al[pl.ds(row, 32), k : k + size] = low

                        @pl.when(slot >= 0)
                        def _():
                            put(slot)

                        @pl.when(zh0 == superblock)
                        def _():
                            put(8 + inner)

            return carry

        lax.fori_loop(0, 4, step, 0)

    fill(far, core0)
    fill(other_far, 1 - core0)


def final_kernel(
    where_ref, structure_ref, high_ref, low_ref, square_ref, ah, al, far, other_far,
    cross_ref, variance_ref, sigma_ref, slot_ref, th, tl, squares,
):
    patch(where_ref, structure_ref, slot_ref, far, other_far, ah, al)
    squares[...] = jnp.zeros_like(squares)

    def times(r, carry):
        k = pl.multiple_of(r * 256, 256)
        live = jnp.int32(0)
        for q in range(4):
            live += (structure_ref[0, 2 * q] < 2 * (r + 1)).astype(jnp.int32)

        @pl.when(live == 0)
        def _():
            zero = jnp.zeros((512, 256), BF16)
            th[:, pl.ds(k, 256)] = zero
            tl[:, pl.ds(k, 256)] = zero

        for v in range(1, 5):
            @pl.when(live == v)
            def _():
                depth = 256 * v
                total = dot3(
                    high_ref[:, :depth], low_ref[:, :depth],
                    ah[:depth, pl.ds(k, 256)], al[:depth, pl.ds(k, 256)], NN,
                )
                high, low = halves(total)
                th[:, pl.ds(k, 256)] = high
                tl[:, pl.ds(k, 256)] = low
                square = total * total
                squares[...] += square[:, :128] + square[:, 128:]

        return carry

    lax.fori_loop(0, 8, times, 0)

    def back(q, carry):
        row = pl.multiple_of(q * 256, 256)
        first = structure_ref[0, 2 * q] // 2
        for v in range(8):
            @pl.when(first == v)
            def _():
                k = 256 * v
                cross_ref[0, pl.ds(row, 256), :] = -dot3(
                    ah[pl.ds(row, 256), k:], al[pl.ds(row, 256), k:], th[:, k:], tl[:, k:], NT
                )

        return carry

    lax.fori_loop(0, 4, back, 0)
    variance_ref[...] = square_ref[...] + jnp.sum(squares[...].T, axis=0, keepdims=True)
    part = (where_ref[2] & 1) * 2 + where_ref[3]
    rows = pl.ds(pl.multiple_of(1536 + part * 32, 32), 32)
    sigma_ref[...] = dot3(ah[1024:1536, :], al[1024:1536, :], ah[rows, :], al[rows, :], NT).T


def final(where, structure, high, low, square, pieces):
    return pl.pallas_call(
        final_kernel,
        out_shape=(
            jax.ShapeDtypeStruct((1, 1024, 512), F32),
            jax.ShapeDtypeStruct((1, 512), F32),
            jax.ShapeDtypeStruct((32, 512), F32),
        ),
        in_specs=[SMEM, SMEM] + [VMEM] * 7,
        out_specs=(VMEM, VMEM, VMEM),
        scratch_shapes=[
            pltpu.SMEM((16,), jnp.int32),
            pltpu.VMEM((512, 2048), BF16), pltpu.VMEM((512, 2048), BF16),
            pltpu.VMEM((512, 128), F32),
        ],
        compiler_params=limit(26),
        cost_estimate=pl.CostEstimate(flops=10**10, bytes_accessed=10 * 2**20, transcendentals=0),
        name="final",
    )(where, structure, high, low, square, *pieces)


def body(root_inverse, child_inverse, child_panel, structure, widths):
    tie = lax.optimization_barrier
    col = lax.axis_index("col")
    zh0 = lax.axis_index("row")
    y0, zl0, x0, core0 = col // 16, (col // 8) % 2, (col // 2) % 4, col % 2
    where = jnp.stack([y0, zl0, x0, core0, zh0]).astype(jnp.int32)

    own = root_inverse.T
    folded = send(own, fold_move)
    moved = ((y0 == 3) & ((zh0 == 1) | (zh0 == 2))) | ((y0 == 2) & (zh0 == 1))
    own = jnp.where(moved, folded, own)
    planes = [own] + [send(own, plane_move(step)) for step in (1, 2, 3)]
    line = make_line(where, planes)

    quad = join([line] + [send(line, first_move(step)) for step in (1, 2, 3)])
    left, right = send(quad, second_move(1)), send(quad, second_move(3))
    quad_z = send(quad, pair_move)
    quad, child_inverse, child_panel = tie((quad, child_inverse, child_panel))
    high, low, square = update(widths, child_inverse, child_panel)
    left, right, quad_z, high, low, square = tie((left, right, quad_z, high, low, square))

    ahead, behind, aside = mix(left, right, quad_z)
    quad, left, right, quad_z, ahead, behind, aside = tie((quad, left, right, quad_z, ahead, behind, aside))
    ahead, behind, aside = send(ahead, second_move(1)), send(behind, second_move(3)), send(aside, pair_move)
    a = join([quad, left, right, quad_z])
    other_a = send(a, core_move)

    ahead_tail, behind_tail = tails(ahead, behind)
    ahead, behind, aside, ahead_tail, behind_tail = tie((ahead, behind, aside, ahead_tail, behind_tail))
    far = [send(ahead_tail, second_move(1)), send(behind_tail, second_move(3))]
    b = join([ahead, behind, aside])
    other_b = send(b, core_move)
    other_b, far = tie((other_b, far))
    ah, al = lay(where, structure, [a, b, other_a, other_b])
    c = join(far)
    other_c = send(c, core_move)
    cross, variance, sigma = final(where, structure, high, low, square, [ah, al, c, other_c])
    return sigma.T, cross, variance


def solution(mesh):
    placed = (
        P("row", "col"),
        P(("col", "row"), None, None),
        P(("col", "row"), None, None),
        P(("col", "row"), None),
        P(("col", "row")),
    )
    return jax.shard_map(
        body,
        mesh=mesh,
        in_specs=placed,
        out_specs=(P("row", "col"), P(("col", "row"), None, None), P(("col", "row"), None)),
        check_vma=False,
    )
```

```python
import itertools

import jax
import jax.numpy as jnp
from jax import lax
from jax.experimental import pallas as pl
from jax.experimental.pallas import tpu as pltpu
from jax.sharding import PartitionSpec as P

AXES = ("col", "row")
F32 = jnp.float32
BF16 = jnp.bfloat16
NN = (((1,), (0,)), ((), ()))
NT = (((1,), (1,)), ((), ()))


def flat(y, zl, x, c, zh):
    return (((y * 2 + zl) * 4 + x) * 2 + c) * 4 + zh


def places():
    return itertools.product(range(4), range(2), range(4), range(2), range(4))


def pairs(move):
    found = []
    for place in places():
        target = move(*place)
        if target is not None:
            found.append((flat(*place), flat(*target)))
    return found


def fold_move(y, zl, x, c, zh):
    swaps = {(0, 1): (3, 1), (0, 2): (3, 2), (1, 2): (2, 1), (3, 1): (0, 1), (3, 2): (0, 2), (2, 1): (1, 2)}
    target = swaps.get((y, zh), (y, zh))
    return (target[0], zl, x, c, target[1])


def plane_move(step):
    return lambda y, zl, x, c, zh: (y, zl, x, c, (zh + step) % 4)


def pair_move(y, zl, x, c, zh):
    z = zh * 2 + zl
    near = z ^ 1 if c == 0 else (z + (1 if z % 2 else -1)) % 8
    return (y, near % 2, x, c, near // 2)


def first_move(step):
    def move(y, zl, x, c, zh):
        return ((y + step) % 4, zl, x, c, zh) if c == 0 else (y, zl, (x + step) % 4, c, zh)

    return move


def second_move(step):
    def move(y, zl, x, c, zh):
        return (y, zl, (x + step) % 4, c, zh) if c == 0 else ((y + step) % 4, zl, x, c, zh)

    return move


def core_move(y, zl, x, c, zh):
    return (y, zl, x, 1 - c, zh)


def send(value, move):
    return lax.ppermute(value, AXES, pairs(move))


def halves(value):
    high = value.astype(BF16)
    return high, (value - high.astype(F32)).astype(BF16)


def dot3(ah, al, bh, bl, dims):
    def one(a, b):
        return lax.dot_general(a, b, dims, preferred_element_type=F32)

    return one(ah, bh) + (one(ah, bl) + one(al, bh))


def update_kernel(width_ref, inverse_ref, panel_ref, high_ref, low_ref, square_ref):
    width = width_ref[0]
    inverse = inverse_ref[0]
    rows = lax.broadcasted_iota(jnp.int32, inverse.shape, 0)
    cols = lax.broadcasted_iota(jnp.int32, inverse.shape, 1)
    inverse = jnp.where((rows < width) & (cols < width), inverse, 0.0)
    square_ref[...] = jnp.sum(inverse * inverse, axis=0, keepdims=True)
    inverse_high, inverse_low = halves(inverse.T)
    for part in range(4):
        panel = panel_ref[0, pl.ds(part * 256, 256), :]
        live = lax.broadcasted_iota(jnp.int32, panel.shape, 1) < width
        panel_high, panel_low = halves(jnp.where(live, panel, 0.0))
        update = dot3(inverse_high, inverse_low, panel_high, panel_low, NT)
        high, low = halves(update)
        high_ref[:, pl.ds(part * 256, 256)] = high
        low_ref[:, pl.ds(part * 256, 256)] = low


def update(widths, child_inverse, child_panel):
    vmem = pl.BlockSpec(memory_space=pltpu.VMEM)
    return pl.pallas_call(
        update_kernel,
        out_shape=(
            jax.ShapeDtypeStruct((512, 1024), BF16),
            jax.ShapeDtypeStruct((512, 1024), BF16),
            jax.ShapeDtypeStruct((1, 512), F32),
        ),
        in_specs=[pl.BlockSpec(memory_space=pltpu.SMEM), vmem, vmem],
        out_specs=(vmem, vmem, vmem),
        compiler_params=pltpu.CompilerParams(vmem_limit_bytes=12 * 2**20),
        cost_estimate=pl.CostEstimate(flops=6 * 1024 * 512 * 512, bytes_accessed=5 * 2**20, transcendentals=0),
        name="update",
    )(widths, child_inverse, child_panel)


VMEM = pl.BlockSpec(memory_space=pltpu.VMEM)
SMEM = pl.BlockSpec(memory_space=pltpu.SMEM)
EARLY, LATE = 768, 512
WIDE = EARLY + LATE


def limit(mebibytes):
    return pltpu.CompilerParams(vmem_limit_bytes=mebibytes * 2**20)


def line_kernel(where_ref, *refs):
    out = refs[-1]
    y0, zh0 = where_ref[0], where_ref[4]
    whole = jnp.minimum(y0, 2)
    half = jnp.where(y0 == 1, 2, 1)
    for d in range(4):
        source = refs[d]
        slot = (zh0 - d) & 3

        @pl.when(slot == 3)
        def _():
            out[:, EARLY:] = source[...]

        @pl.when((slot == whole) & (y0 < 2))
        def _():
            out[:, :512] = source[...]

        @pl.when((slot == half) & (y0 < 2))
        def _():
            out[:, 512:EARLY] = source[:, :256]

        @pl.when((slot == whole) & (y0 >= 2))
        def _():
            out[:, 256:EARLY] = source[...]

        @pl.when((slot == half) & (y0 >= 2))
        def _():
            out[:, :256] = source[:, 256:]


def make_line(where, planes):
    return pl.pallas_call(
        line_kernel,
        out_shape=jax.ShapeDtypeStruct((32, WIDE), F32),
        in_specs=[SMEM] + [VMEM] * 4,
        out_specs=VMEM,
        compiler_params=limit(2),
        name="line",
    )(where, *planes)


def join_kernel(*refs):
    out = refs[-1]
    start = 0
    for source in refs[:-1]:
        count = source.shape[0] if len(source.shape) == 3 else 1
        out[start : start + count] = source[...].reshape((count,) + out.shape[1:])
        start += count


def join(parts):
    count = sum(part.shape[0] if part.ndim == 3 else 1 for part in parts)
    return pl.pallas_call(
        join_kernel,
        out_shape=jax.ShapeDtypeStruct((count,) + parts[0].shape[-2:], F32),
        in_specs=[VMEM] * len(parts),
        out_specs=VMEM,
        compiler_params=limit(6),
        name="join",
    )(*parts)


def mix_kernel(left, right, quad, ahead, behind, aside):
    ahead[:2] = left[:2]
    ahead[2:] = quad[:2]
    behind[:2] = right[2:]
    behind[2:] = quad[2:]
    aside[:2] = left[2:]
    aside[2:] = right[:2]


def mix(left, right, quad):
    shape = jax.ShapeDtypeStruct((4, 32, WIDE), F32)
    return pl.pallas_call(
        mix_kernel,
        out_shape=(shape,) * 3,
        in_specs=[VMEM] * 3,
        out_specs=(VMEM,) * 3,
        compiler_params=limit(5),
        name="mix",
    )(left, right, quad)


def tails_kernel(ahead, behind, ahead_out, behind_out):
    ahead_out[...] = ahead[2:]
    behind_out[...] = behind[2:]


def tails(ahead, behind):
    shape = jax.ShapeDtypeStruct((2, 32, WIDE), F32)
    return pl.pallas_call(
        tails_kernel,
        out_shape=(shape,) * 2,
        in_specs=[VMEM] * 2,
        out_specs=(VMEM,) * 2,
        compiler_params=limit(4),
        name="tails",
    )(ahead, behind)


ROWS = 13 * 128
PLAN = (
    ((0, 768, 0, 0), (0, 768, 3, 768), (768, 512, 0, 1536)),
    ((0, 768, 1, 512), (0, 256, 2, 1280), (768, 512, 1, 1536)),
    ((256, 512, 2, 1024), (768, 512, 2, 1536)),
    ((768, 512, 3, 1536),),
)


def source_of(zr, d2, d1):
    if zr == 0:
        if d2 == 2:
            return (1, d1) if d1 < 2 else (1, 2 + d1)
        return 0, {0: 0, 1: 4, 3: 8}[d2] + d1
    if d2 == 0:
        return 0, 12 + d1
    if d2 == 1:
        return (1, 2 + d1) if d1 < 2 else (1, 6 + d1)
    if d2 == 3:
        return (1, 10 + d1) if d1 < 2 else (1, 4 + d1)
    return 2, d1


def lay_kernel(where_ref, structure_ref, near, side, other_near, other_side, ah, al, block_ref, table_ref):
    y0, zl0, x0, core0, zh0 = (where_ref[i] for i in range(5))
    for t in range(8):
        block_ref[t] = structure_ref[0, t]
    for t in range(4):
        block_ref[8 + t] = zh0 * 4 + t
    block_ref[12] = y0 * 4 + zl0 * 2 + x0 // 2
    for zr, d2, d1 in itertools.product(range(2), range(4), range(4)):
        array, index = source_of(zr, d2, d1)
        table_ref[zr * 16 + d2 * 4 + d1] = array * 16 + index

    def fill(*sources):
        def step(t, carry):
            block = block_ref[t]
            y, inner = block // 4, block & 3
            zr, xb = (inner // 2) ^ zl0, (inner & 1) * 2
            base = pl.multiple_of(t * 128, 128)

            def copy(part, lane, size, group, k):
                core = part & 1
                dy, dx = (y0 - group) & 3, (x0 - xb - part // 2) & 3
                d1, d2 = (dy, dx) if core == 0 else (dx, dy)
                first, second = sources[core]
                code = table_ref[zr * 16 + d2 * 4 + d1]
                index = code & 15
                lanes = slice(lane, lane + size)
                value = jnp.where(
                    code < 16, first[index, :, lanes], second[jnp.minimum(index, 11), :, lanes]
                )
                high, low = halves(value)
                row = pl.multiple_of(base + part * 32, 32)
                ah[pl.ds(row, 32), k : k + size] = high
                al[pl.ds(row, 32), k : k + size] = low

            for superblock in range(4):
                @pl.when(y == superblock)
                def _():
                    if superblock:
                        zero = jnp.zeros((128, 512 * superblock), BF16)
                        ah[pl.ds(base, 128), : 512 * superblock] = zero
                        al[pl.ds(base, 128), : 512 * superblock] = zero
                    for part in range(4):
                        for found in PLAN[superblock]:
                            copy(part, *found)

            return carry

        lax.fori_loop(0, 13, step, 0)

    @pl.when(core0 == 0)
    def _():
        fill((near, side), (other_near, other_side))

    @pl.when(core0 == 1)
    def _():
        fill((other_near, other_side), (near, side))


def lay(where, structure, pieces):
    shape = jax.ShapeDtypeStruct((ROWS, 2048), BF16)
    return pl.pallas_call(
        lay_kernel,
        out_shape=(shape, shape),
        in_specs=[SMEM, SMEM] + [VMEM] * 4,
        out_specs=(VMEM, VMEM),
        scratch_shapes=[pltpu.SMEM((16,), jnp.int32), pltpu.SMEM((32,), jnp.int32)],
        compiler_params=limit(25),
        cost_estimate=pl.CostEstimate(flops=10**10, bytes_accessed=10 * 2**20, transcendentals=0),
        name="lay",
    )(where, structure, *pieces)


FAR_PLAN = (
    ((0, 768, 0, 0), (768, 512, 0, 1536)),
    ((0, 768, 1, 512), (768, 512, 1, 1536)),
    ((0, 256, 1, 1280), (256, 512, 2, 1024), (768, 512, 2, 1536)),
    ((0, 768, 0, 768), (768, 512, 3, 1536)),
)


def patch(where_ref, structure_ref, slot_ref, far, other_far, ah, al):
    y0, zl0, x0, core0, zh0 = (where_ref[i] for i in range(5))
    for block in range(16):
        slot_ref[block] = -1
    for t in range(8):
        slot_ref[structure_ref[0, t]] = t

    def fill(source, core):
        def step(d1, carry):
            y = (y0 - jnp.where(core == 0, d1, 2)) & 3
            x = (x0 - jnp.where(core == 0, 2, d1)) & 3
            inner = (1 - zl0) * 2 + x // 2
            offset = (x & 1) * 64 + core * 32
            for group in range(4):
                @pl.when(y == group)
                def _():
                    for lane, size, superblock, k in FAR_PLAN[group]:
                        slot = slot_ref[superblock * 4 + inner]

                        def put(block):
                            row = pl.multiple_of(block * 128 + offset, 32)
                            high, low = halves(source[d1, :, lane : lane + size])
                            ah[pl.ds(row, 32), k : k + size] = high
                            al[pl.ds(row, 32), k : k + size] = low

                        @pl.when(slot >= 0)
                        def _():
                            put(slot)

                        @pl.when(zh0 == superblock)
                        def _():
                            put(8 + inner)

            return carry

        lax.fori_loop(0, 4, step, 0)

    fill(far, core0)
    fill(other_far, 1 - core0)


def final_kernel(
    where_ref, structure_ref, high_ref, low_ref, square_ref, ah, al, far, other_far,
    cross_ref, variance_ref, sigma_ref, slot_ref, th, tl, squares, result, pair, sums, done,
):
    patch(where_ref, structure_ref, slot_ref, far, other_far, ah, al)
    squares[...] = jnp.zeros_like(squares)

    def times(r, carry):
        k = pl.multiple_of(r * 256, 256)
        live = jnp.int32(0)
        for q in range(4):
            live += (structure_ref[0, 2 * q] < 2 * (r + 1)).astype(jnp.int32)

        @pl.when(live == 0)
        def _():
            zero = jnp.zeros((512, 256), BF16)
            th[:, pl.ds(k, 256)] = zero
            tl[:, pl.ds(k, 256)] = zero

        for v in range(1, 5):
            @pl.when(live == v)
            def _():
                depth = 256 * v
                total = dot3(
                    high_ref[:, :depth], low_ref[:, :depth],
                    ah[:depth, pl.ds(k, 256)], al[:depth, pl.ds(k, 256)], NN,
                )
                high, low = halves(total)
                th[:, pl.ds(k, 256)] = high
                tl[:, pl.ds(k, 256)] = low
                square = total * total
                squares[...] += square[:, :128] + square[:, 128:]

        return carry

    lax.fori_loop(0, 8, times, 0)

    def back(q, carry):
        row = pl.multiple_of(q * 256, 256)
        first = structure_ref[0, 2 * q] // 2
        for v in range(8):
            @pl.when(first == v)
            def _():
                k = 256 * v
                result[pl.ds(row, 256), :] = -dot3(
                    ah[pl.ds(row, 256), k:], al[pl.ds(row, 256), k:], th[:, k:], tl[:, k:], NT
                )

        leave(q).start()
        return carry

    def leave(q):
        rows = pl.ds(pl.multiple_of(q * 256, 256), 256)
        return pltpu.make_async_copy(result.at[rows, :], cross_ref.at[0, rows, :], done.at[q])

    lax.fori_loop(0, 4, back, 0)
    variance_ref[...] = square_ref[...] + jnp.sum(squares[...].T, axis=0, keepdims=True)
    part = (where_ref[2] & 1) * 2 + where_ref[3]
    rows = pl.ds(pl.multiple_of(1536 + part * 32, 32), 32)
    pair[:32] = ah[rows, :]
    pair[32:] = al[rows, :]
    for v in range(4):
        @pl.when(jnp.maximum(where_ref[0], where_ref[4]) == v)
        def _():
            k = 512 * v
            wide = lax.dot_general(ah[1024:1536, k:], pair[:, k:], NT, preferred_element_type=F32)
            rest = lax.dot_general(al[1024:1536, k:], pair[:32, k:], NT, preferred_element_type=F32)
            sums[...] = wide[:, :32] + (wide[:, 32:] + rest)

    sigma_ref[...] = sums[...].T
    for q in range(4):
        leave(q).wait()


def final(where, structure, high, low, square, pieces):
    return pl.pallas_call(
        final_kernel,
        out_shape=(
            jax.ShapeDtypeStruct((1, 1024, 512), F32),
            jax.ShapeDtypeStruct((1, 512), F32),
            jax.ShapeDtypeStruct((32, 512), F32),
        ),
        in_specs=[SMEM, SMEM] + [VMEM] * 7,
        out_specs=(pl.BlockSpec(memory_space=pl.ANY), VMEM, VMEM),
        scratch_shapes=[
            pltpu.SMEM((16,), jnp.int32),
            pltpu.VMEM((512, 2048), BF16), pltpu.VMEM((512, 2048), BF16),
            pltpu.VMEM((512, 128), F32), pltpu.VMEM((1024, 512), F32),
            pltpu.VMEM((64, 2048), BF16), pltpu.VMEM((512, 32), F32),
            pltpu.SemaphoreType.DMA((4,)),
        ],
        compiler_params=limit(26),
        cost_estimate=pl.CostEstimate(flops=10**10, bytes_accessed=10 * 2**20, transcendentals=0),
        name="final",
    )(where, structure, high, low, square, *pieces)


def body(root_inverse, child_inverse, child_panel, structure, widths):
    tie = lax.optimization_barrier
    col = lax.axis_index("col")
    zh0 = lax.axis_index("row")
    y0, zl0, x0, core0 = col // 16, (col // 8) % 2, (col // 2) % 4, col % 2
    where = jnp.stack([y0, zl0, x0, core0, zh0]).astype(jnp.int32)

    own = root_inverse.T
    folded = send(own, fold_move)
    moved = ((y0 == 3) & ((zh0 == 1) | (zh0 == 2))) | ((y0 == 2) & (zh0 == 1))
    own = jnp.where(moved, folded, own)
    planes = [own] + [send(own, plane_move(step)) for step in (1, 2, 3)]
    line = make_line(where, planes)

    quad = join([line] + [send(line, first_move(step)) for step in (1, 2, 3)])
    left, right = send(quad, second_move(1)), send(quad, second_move(3))
    quad_z = send(quad, pair_move)
    quad, child_inverse, child_panel = tie((quad, child_inverse, child_panel))
    high, low, square = update(widths, child_inverse, child_panel)
    left, right, quad_z, high, low, square = tie((left, right, quad_z, high, low, square))

    ahead, behind, aside = mix(left, right, quad_z)
    quad, left, right, quad_z, ahead, behind, aside = tie((quad, left, right, quad_z, ahead, behind, aside))
    ahead, behind, aside = send(ahead, second_move(1)), send(behind, second_move(3)), send(aside, pair_move)
    a = join([quad, left, right, quad_z])
    other_a = send(a, core_move)

    ahead_tail, behind_tail = tails(ahead, behind)
    ahead, behind, aside, ahead_tail, behind_tail = tie((ahead, behind, aside, ahead_tail, behind_tail))
    far = [send(ahead_tail, second_move(1)), send(behind_tail, second_move(3))]
    b = join([ahead, behind, aside])
    other_b = send(b, core_move)
    other_b, far = tie((other_b, far))
    ah, al = lay(where, structure, [a, b, other_a, other_b])
    c = join(far)
    other_c = send(c, core_move)
    cross, variance, sigma = final(where, structure, high, low, square, [ah, al, c, other_c])
    return sigma.T, cross, variance


def solution(mesh):
    placed = (
        P("row", "col"),
        P(("col", "row"), None, None),
        P(("col", "row"), None, None),
        P(("col", "row"), None),
        P(("col", "row")),
    )
    return jax.shard_map(
        body,
        mesh=mesh,
        in_specs=placed,
        out_specs=(P("row", "col"), P(("col", "row"), None, None), P(("col", "row"), None)),
        check_vma=False,
    )
```
